32 devices in a mesh: sub: 8 (over y, x, core), row: 4 (over z).
Axes of the slice: x: 2, y: 2, z: 4, core: 2. Of those that a mesh axis runs over, the one named last changes fastest.
Arguments:
- sigma_top: float32 [6144, 6144], P('row', 'sub'), may hold values from -2 to 4, as said below
- coupling: float32 [8, 6144, 768], P('sub', 'row'), may hold values from -0.16 to 0.16
- child_inverse: float32 [8, 768, 768], P('sub', 'row'), may hold values from -1 to 10, as said below
- tile_mask: int32 [8, 24], P('sub'), may hold values 0 or 1
- obs_node: int32 [8192], P(('sub', 'row')), may hold values from 0 to 6143
- obs_noise: float32 [8192], P(('sub', 'row')), may hold values from 0.05 to 2
Outputs:
- sep_child: float32 [8, 6144, 768], P('sub', 'row')
- child_block: float32 [8, 768, 768], P('sub', 'row')
- loo_var: float32 [8192], P(('sub', 'row'))
The draws below stay inside these ranges and needn't reach their ends.
Inputs may be any that keep to these rules, and one draw needn't show every extreme that they name: sigma_top is exactly symmetric. Each child_inverse[c] is exactly symmetric.
All inputs are finite; a program needn't handle non-finite values. No bound on the sum of `tile_mask` on one device may be relied on, other than what follows from the above.
Results may differ from the reference program's by a relative error of at most 0.000073.
Values sent between devices are 32-bit elements; how exact they have to be, the bound alone decides.
A program may use at most 128 MiB of HBM per device.

```python
import math
import jax
import jax.numpy as jnp
from jax import lax

TILE = 256
ST = 24
CW = 768
SEP = 6144
CHILDREN = 8
NOBS = 8192


def draw_sigma_top(key, part):
    size_all = ST * TILE
    key_a, key_b = jax.random.split(jax.random.fold_in(key, 11), 2)
    raw = jnp.clip(jax.random.normal(key_a, (size_all, size_all), jnp.float32), -4.0, 4.0)
    coeff = 0.4 / size_all ** 0.5
    sym = (raw + raw.T) * coeff
    diag_vals = jax.random.uniform(key_b, (size_all,), jnp.float32, 1.5, 2.5)
    ident = lax_iota_eq(size_all).astype(jnp.float32)
    return sym * (1.0 - ident) + ident * diag_vals[:, None]


def lax_iota_eq(size_all):
    idx = jnp.arange(size_all, dtype=jnp.int32)
    return idx[:, None] == idx[None, :]


def draw_child_inverse(key, part):
    key_a, key_b = jax.random.split(jax.random.fold_in(key, 23), 2)
    raw = jnp.clip(jax.random.normal(key_a, (CHILDREN, CW, CW), jnp.float32), -4.0, 4.0)
    sym = (raw + jnp.swapaxes(raw, 1, 2)) * (0.5 / CW ** 0.5)
    diag_vals = jax.random.uniform(key_b, (CHILDREN, CW), jnp.float32, 6.0, 10.0)
    ident = lax_iota_eq(CW).astype(jnp.float32)
    return sym * (1.0 - ident)[None] + ident[None] * diag_vals[:, :, None]


def touch_ends(entries, own_key, smallest, top_value):
    shape = entries.shape
    place = [jax.random.randint(jax.random.fold_in(own_key, axis), (), 0, shape[axis]) for axis in range(len(shape))]
    entries = entries.at[tuple(place)].set(smallest)
    longest = shape.index(max(shape))
    place[longest] = (place[longest] + 1) % shape[longest]
    return entries.at[tuple(place)].set(top_value)


def steps_of(rng, dims, shards, smallest, high):
    def one(dim, parts):
        heights = jax.random.uniform(jax.random.fold_in(jax.random.fold_in(rng, 6), dim), (parts,), jnp.float32, smallest / len(shards), high / len(shards))
        return jnp.repeat(jnp.exp(heights), dims[dim] // parts).reshape((-1,) + (1,) * (len(dims) - dim - 1))

    factor_of = one(*shards[0])
    for cut in shards[1:]:
        factor_of = factor_of * one(*cut)
    return factor_of


def scatter_about(stream_key, shape, scale, reach, pieces=(), held_as=jnp.bfloat16):
    drawn = jax.random.normal(stream_key, shape, jnp.float32) * scale
    if len(pieces) > 0:
        drawn = steps_of(stream_key, shape, pieces, -0.22, 0.18) * drawn
    return jnp.clip(drawn, min=-reach, max=reach).astype(held_as)


def setup_inputs(seed: int = 0) -> dict:
    key_list = jax.random.split(jax.random.key(seed), 7)
    return {
        "sigma_top": draw_sigma_top(jax.random.fold_in(key_list[6], 71), 0),
        "coupling": scatter_about(key_list[1], (CHILDREN, SEP, CW), 0.025, 0.16, ((0, 8), (1, 4)), jnp.float32),
        "child_inverse": draw_child_inverse(jax.random.fold_in(key_list[6], 71), 0),
        "tile_mask": touch_ends((jax.random.randint(key_list[3], (CHILDREN, ST), 0, 8) < 5).astype(jnp.int32), jax.random.fold_in(key_list[3], 1), 0, 1),
        "obs_node": touch_ends(jax.random.randint(key_list[4], (NOBS,), 0, CHILDREN * CW), jax.random.fold_in(key_list[4], 1), 0, (CHILDREN * CW) - 1).astype(jnp.int32),
        "obs_noise": jnp.clip(jnp.exp(math.log(2.0) - 3.6888794 * jax.random.uniform(key_list[5], (NOBS,), jnp.float32) ** steps_of(key_list[5], (NOBS,), ((0, 32),), -0.2, 0.2)), 0.05, 2.0),
    }


def reference(sigma_top, coupling, child_inverse, tile_mask, obs_node, obs_noise):
    highest = lax.Precision.HIGHEST
    row_mask = jnp.repeat(tile_mask, TILE, axis=1).astype(jnp.float32)
    masked = coupling * row_mask[:, :, None]

    def per_child(pair):
        coupled, inverse = pair
        product = jnp.dot(sigma_top, coupled, precision=highest, preferred_element_type=jnp.float32)
        sep_part = -product
        update = jnp.dot(coupled.T, sep_part, precision=highest, preferred_element_type=jnp.float32)
        return sep_part, inverse - update

    sep_child, child_block = lax.map(per_child, (masked, child_inverse))
    variances = jnp.diagonal(child_block, axis1=1, axis2=2).reshape(-1)
    loo_var = variances[obs_node] + obs_noise
    return sep_child, child_block, loo_var
```

```python
import functools
import jax
import jax.numpy as jnp
from jax import lax
from jax.experimental import pallas as pl
from jax.experimental.pallas import tpu as pltpu
from jax.sharding import PartitionSpec as P

TILE = 256
STRIP = 128
MESH = pl.DeviceIdType.MESH


def flip(index, bits, size):
    total, step = 0, 1
    while step < size:
        digit = (index // step) % 2
        if (bits // step) % 2:
            digit = 1 - digit
        total = total + digit * step
        step *= 2
    return total


def halves(x):
    high = x.astype(jnp.bfloat16)
    low = (x - high.astype(jnp.float32)).astype(jnp.bfloat16)
    return high, low


def gather_multiply(
    subs, rows, mask_ref, s_ref, m_ref, out_ref, s_all, m_all,
    s_tile, m_tile, m_high, m_low,
    s_send, s_pass, s_recv, m_up, m_down, m_recv, load_sem, own_sem,
):
    sub, row = lax.axis_index("sub"), lax.axis_index("row")
    chips = subs // 2
    chip, core = sub // 2, sub % 2
    mate = chip * 2 + (1 - core)
    height, depth = s_ref.shape
    per = height // depth
    strips = depth // STRIP
    rt = 512 if height % 512 == 0 else 256

    def peer(x):
        return flip(chip, x, chips) * 2 + core

    barrier = pltpu.get_barrier_semaphore()
    for x in range(1, chips):
        pl.semaphore_signal(barrier, inc=1, device_id=(peer(x), row), device_id_type=MESH)
    pl.semaphore_signal(barrier, inc=1, device_id=(mate, row), device_id_type=MESH)

    @pl.when(row > 0)
    def _():
        pl.semaphore_signal(barrier, inc=1, device_id=(sub, row - 1), device_id_type=MESH)

    @pl.when(row < rows - 1)
    def _():
        pl.semaphore_signal(barrier, inc=1, device_id=(sub, row + 1), device_id_type=MESH)

    @pl.when((row > 0) & (row < rows - 1))
    def _():
        pl.semaphore_wait(barrier, chips + 2)

    @pl.when((row == 0) | (row == rows - 1))
    def _():
        pl.semaphore_wait(barrier, chips + 1)

    def m_copy(src, j, up):
        return pltpu.make_async_remote_copy(
            src_ref=src, dst_ref=m_all.at[j],
            send_sem=(m_up if up else m_down).at[j], recv_sem=m_recv.at[j],
            device_id=(sub, row + 1 if up else row - 1), device_id_type=MESH,
        )

    def s_copy(x):
        return pltpu.make_async_remote_copy(
            src_ref=s_ref, dst_ref=s_all.at[sub],
            send_sem=s_send.at[x], recv_sem=s_recv.at[sub],
            device_id=(peer(x), row), device_id_type=MESH,
        )

    def s_pass_on(x):
        block = peer(x)
        return pltpu.make_async_remote_copy(
            src_ref=s_ref if x == 0 else s_all.at[block], dst_ref=s_all.at[block],
            send_sem=s_pass.at[x], recv_sem=s_recv.at[block],
            device_id=(mate, row), device_id_type=MESH,
        )

    def s_arrived(block):
        return pltpu.make_async_remote_copy(
            src_ref=s_all.at[block], dst_ref=s_all.at[block],
            send_sem=s_send.at[0], recv_sem=s_recv.at[block],
            device_id=(mate, row), device_id_type=MESH,
        )

    def m_arrived(j):
        return pltpu.make_async_remote_copy(
            src_ref=m_all.at[j], dst_ref=m_all.at[j],
            send_sem=m_up.at[j], recv_sem=m_recv.at[j],
            device_id=(mate, row), device_id_type=MESH,
        )

    for h in range(per):
        @pl.when(row < rows - 1)
        def _():
            m_copy(m_ref.at[h], row * per + h, True).start()

        @pl.when(row > 0)
        def _():
            m_copy(m_ref.at[h], row * per + h, False).start()
    for x in range(1, chips):
        s_copy(x).start()
    s_pass_on(0).start()

    own_s = pltpu.make_async_copy(s_ref, s_all.at[sub], own_sem.at[0])
    own_m = pltpu.make_async_copy(m_ref, m_all.at[pl.ds(row * per, per)], own_sem.at[1])
    own_s.start()
    own_m.start()
    out_ref[...] = jnp.zeros_like(out_ref)
    own_s.wait()
    own_m.wait()

    def receive(distance, h, then):
        for sign in (1, -1):
            block = row + sign * distance

            @pl.when((block >= 0) & (block < rows))
            def _():
                j = block * per + h
                m_arrived(j).wait_recv()
                if sign == 1:
                    @pl.when(row > 0)
                    def _():
                        m_copy(m_all.at[j], j, False).start()
                else:
                    @pl.when(row < rows - 1)
                    def _():
                        m_copy(m_all.at[j], j, True).start()
                if then is not None:
                    then(j)

    def multiply(j):
        load_s = pltpu.make_async_copy(s_all.at[j], s_tile, load_sem.at[0])
        load_m = pltpu.make_async_copy(m_all.at[j], m_tile, load_sem.at[1])
        load_s.start()
        load_m.start()
        load_m.wait()

        @pl.loop(0, strips)
        def _(i):
            part = pl.ds(pl.multiple_of(i * STRIP, STRIP), STRIP)
            high, low = halves(m_tile[part, :] * mask_ref[j * strips + i][0:1, :])
            m_high[part, :] = high
            m_low[part, :] = low

        load_s.wait()

        @pl.loop(0, height // rt)
        def _(i):
            part = pl.ds(pl.multiple_of(i * rt, rt), rt)
            high, low = halves(s_tile[part, :])
            out_ref[part, :] += (
                jnp.dot(high, m_low[...], preferred_element_type=jnp.float32)
                + jnp.dot(low, m_high[...], preferred_element_type=jnp.float32)
                + jnp.dot(high, m_high[...], preferred_element_type=jnp.float32)
            )

    near = min(2, rows - 2)
    for h in range(per):
        receive(1, h, None)
    for x in range(1, chips):
        s_arrived(peer(x)).wait_recv()
        s_pass_on(x).start()
    for distance in range(2, near + 1):
        for h in range(per):
            receive(distance, h, None)
    for x in range(chips):
        s_arrived(flip(chip, x, chips) * 2 + (1 - core)).wait_recv()

    @pl.loop(0, subs)
    def _(j):
        block = j // per

        @pl.when((block - row <= near) & (row - block <= near))
        def _():
            multiply(j)

    @pl.loop(0, (rows - 1 - near) * per)
    def _(n):
        receive(near + 1 + n // per, n % per, multiply)

    for x in range(1, chips):
        s_copy(x).wait_send()
    for x in range(chips):
        s_pass_on(x).wait_send()

    @pl.loop(0, subs)
    def _(j):
        block = j // per

        @pl.when((row < rows - 1) & (block <= row))
        def _():
            m_copy(m_all.at[j], j, True).wait_send()

        @pl.when((row > 0) & (block >= row))
        def _():
            m_copy(m_all.at[j], j, False).wait_send()


def product_here(subs, rows, sigma_top, coupling, tile_mask):
    height, depth = sigma_top.shape
    width = coupling.shape[1]
    per = height // depth
    f32 = jnp.float32
    strips = jnp.repeat(tile_mask, TILE // STRIP).astype(f32)
    strips = jnp.broadcast_to(strips[:, None, None], (strips.shape[0], 8, width))
    whole = pl.BlockSpec(memory_space=pltpu.VMEM)
    hbm = pl.BlockSpec(memory_space=pl.ANY)
    dma = pltpu.SemaphoreType.DMA
    return pl.pallas_call(
        functools.partial(gather_multiply, subs, rows),
        out_shape=(
            jax.ShapeDtypeStruct((height, width), f32),
            jax.ShapeDtypeStruct((subs, height, depth), f32),
            jax.ShapeDtypeStruct((subs, depth, width), f32),
        ),
        in_specs=[whole, hbm, hbm],
        out_specs=(whole, hbm, hbm),
        scratch_shapes=[
            pltpu.VMEM((height, depth), f32),
            pltpu.VMEM((depth, width), f32),
            pltpu.VMEM((depth, width), jnp.bfloat16),
            pltpu.VMEM((depth, width), jnp.bfloat16),
            dma((subs // 2,)),
            dma((subs // 2,)),
            dma((subs,)),
            dma((subs,)),
            dma((subs,)),
            dma((subs,)),
            dma((2,)),
            dma((2,)),
        ],
        compiler_params=pltpu.CompilerParams(
            collective_id=0, has_side_effects=True, vmem_limit_bytes=56 * 2**20
        ),
        cost_estimate=pl.CostEstimate(
            flops=6 * height * subs * depth * width,
            bytes_accessed=8 * (height + width) * subs * depth,
            transcendentals=0,
        ),
    )(strips, sigma_top, coupling.reshape(per, depth, width))[0]


def local(subs, rows, sigma_top, coupling, child_inverse, tile_mask, obs_node, obs_noise):
    rows_here = coupling.shape[1]
    width_here = child_inverse.shape[1]
    tiles_here = rows_here // TILE
    row_index = lax.axis_index("row")
    mask_here = lax.dynamic_slice_in_dim(tile_mask[0], row_index * tiles_here, tiles_here)
    row_mask = jnp.repeat(mask_here, TILE).astype(jnp.float32)
    masked = coupling[0] * row_mask[:, None]
    sep_part = -product_here(subs, rows, sigma_top, coupling[0], tile_mask[0])
    update = lax.psum_scatter(
        lax.dot_general(
            masked,
            sep_part,
            (((0,), (0,)), ((), ())),
            precision=lax.Precision.HIGH,
            preferred_element_type=jnp.float32,
        ),
        "row",
        scatter_dimension=0,
        tiled=True,
    )
    block_here = child_inverse[0] - update
    own_cols = lax.dynamic_slice_in_dim(block_here, row_index * width_here, width_here, 1)
    own_diag = jnp.diagonal(own_cols)
    every_var = lax.all_gather(own_diag, ("sub", "row"), axis=0, tiled=True)
    loo_var = every_var[obs_node] + obs_noise
    return (sep_part[None], block_here[None], loo_var)


def solution(mesh):
    placed = (
        P("row", "sub"),
        P("sub", "row", None),
        P("sub", "row", None),
        P("sub", None),
        P(("sub", "row")),
        P(("sub", "row")),
    )
    return jax.shard_map(
        functools.partial(local, mesh.shape["sub"], mesh.shape["row"]),
        mesh=mesh,
        in_specs=placed,
        out_specs=(P("sub", "row", None), P("sub", "row", None), P(("sub", "row"))),
        check_vma=False,
    )
```

```python
import functools
import jax
import jax.numpy as jnp
from jax import lax
from jax.experimental import pallas as pl
from jax.experimental.pallas import tpu as pltpu
from jax.sharding import PartitionSpec as P

TILE = 256
STRIP = 128
MESH = pl.DeviceIdType.MESH


def flip(index, bits, size):
    total, step = 0, 1
    while step < size:
        digit = (index // step) % 2
        if (bits // step) % 2:
            digit = 1 - digit
        total = total + digit * step
        step *= 2
    return total


def halves(x):
    high = x.astype(jnp.bfloat16)
    low = (x - high.astype(jnp.float32)).astype(jnp.bfloat16)
    return high, low


def gather_multiply(
    subs, rows, mask_ref, s_ref, m_ref, out_ref, s_all, m_all,
    s_tile, m_tile, m_high, m_low,
    s_send, s_pass, s_recv, m_up, m_down, m_recv, load_sem, own_sem,
):
    sub, row = lax.axis_index("sub"), lax.axis_index("row")
    chips = subs // 2
    chip, core = sub // 2, sub % 2
    mate = chip * 2 + (1 - core)
    height, depth = s_ref.shape
    per = height // depth
    strips = depth // STRIP
    rt = 512 if height % 512 == 0 else 256
    half = height // 2
    bits = [1 << n for n in range(chips.bit_length() - 1)]
    spots = {bit: n for n, bit in enumerate(bits)}

    def onward(x, h):
        if x == 0:
            return bits if h == 0 else bits[::-1]
        return [bit for bit in bits if (bit > x if h == 0 else 2 * bit <= (x & -x))]

    def apart(index):
        return sum((index // bit + chip // bit) % 2 for bit in bits)

    def peer(x):
        return flip(chip, x, chips) * 2 + core

    barrier = pltpu.get_barrier_semaphore()
    for x in bits:
        pl.semaphore_signal(barrier, inc=1, device_id=(peer(x), row), device_id_type=MESH)
    pl.semaphore_signal(barrier, inc=1, device_id=(mate, row), device_id_type=MESH)

    @pl.when(row > 0)
    def _():
        pl.semaphore_signal(barrier, inc=1, device_id=(sub, row - 1), device_id_type=MESH)

    @pl.when(row < rows - 1)
    def _():
        pl.semaphore_signal(barrier, inc=1, device_id=(sub, row + 1), device_id_type=MESH)

    @pl.when((row > 0) & (row < rows - 1))
    def _():
        pl.semaphore_wait(barrier, len(bits) + 3)

    @pl.when((row == 0) | (row == rows - 1))
    def _():
        pl.semaphore_wait(barrier, len(bits) + 2)

    def m_copy(src, j, up):
        return pltpu.make_async_remote_copy(
            src_ref=src, dst_ref=m_all.at[j],
            send_sem=(m_up if up else m_down).at[j], recv_sem=m_recv.at[j],
            device_id=(sub, row + 1 if up else row - 1), device_id_type=MESH,
        )

    def s_half(ref, h):
        return ref.at[pl.ds(h * half, half)]

    def s_copy(x, bit, h):
        block = peer(x)
        return pltpu.make_async_remote_copy(
            src_ref=s_half(s_ref if x == 0 else s_all.at[block], h),
            dst_ref=s_half(s_all.at[block], h),
            send_sem=s_send.at[x, spots[bit], h], recv_sem=s_recv.at[block, h],
            device_id=(peer(bit), row), device_id_type=MESH,
        )

    def s_pass_on(x, h):
        block = peer(x)
        return pltpu.make_async_remote_copy(
            src_ref=s_half(s_ref if x == 0 else s_all.at[block], h),
            dst_ref=s_half(s_all.at[block], h),
            send_sem=s_pass.at[x, h], recv_sem=s_recv.at[block, h],
            device_id=(mate, row), device_id_type=MESH,
        )

    def s_arrived(block, h):
        return pltpu.make_async_remote_copy(
            src_ref=s_half(s_all.at[block], h), dst_ref=s_half(s_all.at[block], h),
            send_sem=s_pass.at[0, h], recv_sem=s_recv.at[block, h],
            device_id=(mate, row), device_id_type=MESH,
        )

    def s_receive(x, h):
        s_arrived(peer(x), h).wait_recv()
        for bit in onward(x, h):
            s_copy(x, bit, h).start()
        s_pass_on(x, h).start()

    def from_mate(x):
        for h in range(2):
            s_arrived(flip(chip, x, chips) * 2 + (1 - core), h).wait_recv()

    def m_arrived(j):
        return pltpu.make_async_remote_copy(
            src_ref=m_all.at[j], dst_ref=m_all.at[j],
            send_sem=m_up.at[j], recv_sem=m_recv.at[j],
            device_id=(mate, row), device_id_type=MESH,
        )

    for h in range(per):
        @pl.when(row < rows - 1)
        def _():
            m_copy(m_ref.at[h], row * per + h, True).start()

        @pl.when(row > 0)
        def _():
            m_copy(m_ref.at[h], row * per + h, False).start()

        if h == 0:
            for n in range(2):
                for bit in bits:
                    s_copy(0, bit, n if bit == bits[0] else 1 - n).start()
            for n in range(2):
                s_pass_on(0, n).start()

    own_s = pltpu.make_async_copy(s_ref, s_all.at[sub], own_sem.at[0])
    own_m = pltpu.make_async_copy(m_ref, m_all.at[pl.ds(row * per, per)], own_sem.at[1])
    own_s.start()
    own_m.start()
    out_ref[...] = jnp.zeros_like(out_ref)
    own_s.wait()
    own_m.wait()

    def receive(distance, h, then):
        for sign in (1, -1):
            block = row + sign * distance

            @pl.when((block >= 0) & (block < rows))
            def _():
                j = block * per + h
                m_arrived(j).wait_recv()
                if sign == 1:
                    @pl.when(row > 0)
                    def _():
                        m_copy(m_all.at[j], j, False).start()
                else:
                    @pl.when(row < rows - 1)
                    def _():
                        m_copy(m_all.at[j], j, True).start()
                if then is not None:
                    then(j)

    def multiply(j):
        load_s = pltpu.make_async_copy(s_all.at[j], s_tile, load_sem.at[0])
        load_m = pltpu.make_async_copy(m_all.at[j], m_tile, load_sem.at[1])
        load_s.start()
        load_m.start()
        load_m.wait()

        @pl.loop(0, strips)
        def _(i):
            part = pl.ds(pl.multiple_of(i * STRIP, STRIP), STRIP)
            high, low = halves(m_tile[part, :] * mask_ref[j * strips + i][0:1, :])
            m_high[part, :] = high
            m_low[part, :] = low

        load_s.wait()

        @pl.loop(0, height // rt)
        def _(i):
            part = pl.ds(pl.multiple_of(i * rt, rt), rt)
            high, low = halves(s_tile[part, :])
            out_ref[part, :] += (
                jnp.dot(high, m_low[...], preferred_element_type=jnp.float32)
                + jnp.dot(low, m_high[...], preferred_element_type=jnp.float32)
                + jnp.dot(high, m_high[...], preferred_element_type=jnp.float32)
            )

    def sweep(chosen):
        @pl.loop(0, subs)
        def _(j):
            block = j // per
            distance = jnp.maximum(block - row, row - block)

            @pl.when(chosen(distance, apart(j // 2)))
            def _():
                multiply(j)

    near = min(2, rows - 2)
    close = [x for x in range(1, chips) if x in bits]
    remote = sorted((x for x in range(1, chips) if x not in bits), key=lambda x: x.bit_count())
    for n in range(2):
        for x in close:
            s_receive(x, n if x == bits[0] else 1 - n)
        for h in range(n, per, 2):
            receive(1, h, None)
    from_mate(0)
    for x in close:
        from_mate(x)
    sweep(lambda distance, hops: (distance == 0) & (hops <= 1))
    for x in remote:
        for h in range(2):
            s_receive(x, h)
    if near > 1:
        receive(2, 0, None)
    sweep(lambda distance, hops: (distance == 1) & (hops <= 1))
    if near > 1:
        for h in range(1, per):
            receive(2, h, None)
    for x in remote:
        from_mate(x)
    sweep(lambda distance, hops: (distance <= near) & ((distance > 1) | (hops > 1)))

    @pl.loop(0, (rows - 1 - near) * per)
    def _(n):
        receive(near + 1 + n // per, n % per, multiply)

    for x in range(chips):
        for h in range(2):
            for bit in onward(x, h):
                s_copy(x, bit, h).wait_send()
            s_pass_on(x, h).wait_send()

    @pl.loop(0, subs)
    def _(j):
        block = j // per

        @pl.when((row < rows - 1) & (block <= row))
        def _():
            m_copy(m_all.at[j], j, True).wait_send()

        @pl.when((row > 0) & (block >= row))
        def _():
            m_copy(m_all.at[j], j, False).wait_send()


def product_here(subs, rows, sigma_top, coupling, tile_mask):
    height, depth = sigma_top.shape
    width = coupling.shape[1]
    per = height // depth
    f32 = jnp.float32
    strips = jnp.repeat(tile_mask, TILE // STRIP).astype(f32)
    strips = jnp.broadcast_to(strips[:, None, None], (strips.shape[0], 8, width))
    whole = pl.BlockSpec(memory_space=pltpu.VMEM)
    hbm = pl.BlockSpec(memory_space=pl.ANY)
    dma = pltpu.SemaphoreType.DMA
    return pl.pallas_call(
        functools.partial(gather_multiply, subs, rows),
        out_shape=(
            jax.ShapeDtypeStruct((height, width), f32),
            jax.ShapeDtypeStruct((subs, height, depth), f32),
            jax.ShapeDtypeStruct((subs, depth, width), f32),
        ),
        in_specs=[whole, hbm, hbm],
        out_specs=(whole, hbm, hbm),
        scratch_shapes=[
            pltpu.VMEM((height, depth), f32),
            pltpu.VMEM((depth, width), f32),
            pltpu.VMEM((depth, width), jnp.bfloat16),
            pltpu.VMEM((depth, width), jnp.bfloat16),
            dma((subs // 2, subs.bit_length(), 2)),
            dma((subs // 2, 2)),
            dma((subs, 2)),
            dma((subs,)),
            dma((subs,)),
            dma((subs,)),
            dma((2,)),
            dma((2,)),
        ],
        compiler_params=pltpu.CompilerParams(
            collective_id=0, has_side_effects=True, vmem_limit_bytes=56 * 2**20
        ),
        cost_estimate=pl.CostEstimate(
            flops=6 * height * subs * depth * width,
            bytes_accessed=8 * (height + width) * subs * depth,
            transcendentals=0,
        ),
    )(strips, sigma_top, coupling.reshape(per, depth, width))[0]


def share(subs, rows, own_ref, all_ref, row_send, row_recv, sub_send, sub_recv):
    sub, row = lax.axis_index("sub"), lax.axis_index("row")
    barrier = pltpu.get_barrier_semaphore()
    row_peers = [(sub, (row + d) % rows) for d in range(1, rows)]
    sub_peers = [((sub + d) % subs, row) for d in range(1, subs)]
    for peer in row_peers + sub_peers:
        pl.semaphore_signal(barrier, inc=1, device_id=peer, device_id_type=MESH)
    pl.semaphore_wait(barrier, rows + subs - 2)
    all_ref[pl.ds(sub, 1), pl.ds(row, 1)] = own_ref[...][None, None]

    def along_row(d):
        return pltpu.make_async_remote_copy(
            src_ref=own_ref, dst_ref=all_ref.at[sub, row],
            send_sem=row_send.at[d], recv_sem=row_recv.at[d],
            device_id=row_peers[d], device_id_type=MESH,
        )

    def along_sub(d):
        return pltpu.make_async_remote_copy(
            src_ref=all_ref.at[sub], dst_ref=all_ref.at[sub],
            send_sem=sub_send.at[d], recv_sem=sub_recv.at[d],
            device_id=sub_peers[d], device_id_type=MESH,
        )

    for d in range(rows - 1):
        along_row(d).start()
    for d in range(rows - 1):
        along_row(d).wait()
    for d in range(subs - 1):
        along_sub(d).start()
    for d in range(subs - 1):
        along_sub(d).wait()


def every_variance(subs, rows, own):
    count = own.shape[0]
    lanes = -(-count // STRIP) * STRIP
    padded = jnp.broadcast_to(jnp.pad(own, (0, lanes - count)), (8, lanes))
    whole = pl.BlockSpec(memory_space=pltpu.VMEM)
    dma = pltpu.SemaphoreType.DMA
    shared = pl.pallas_call(
        functools.partial(share, subs, rows),
        out_shape=jax.ShapeDtypeStruct((subs, rows, 8, lanes), jnp.float32),
        in_specs=[whole],
        out_specs=whole,
        scratch_shapes=[
            dma((rows - 1,)), dma((rows - 1,)), dma((subs - 1,)), dma((subs - 1,)),
        ],
        compiler_params=pltpu.CompilerParams(
            collective_id=1, has_side_effects=True, vmem_limit_bytes=16 * 2**20
        ),
    )(padded)
    return shared[:, :, 0, :count].reshape(-1)


def local(subs, rows, sigma_top, coupling, child_inverse, tile_mask, obs_node, obs_noise):
    rows_here = coupling.shape[1]
    width_here = child_inverse.shape[1]
    tiles_here = rows_here // TILE
    row_index = lax.axis_index("row")
    mask_here = lax.dynamic_slice_in_dim(tile_mask[0], row_index * tiles_here, tiles_here)
    row_mask = jnp.repeat(mask_here, TILE).astype(jnp.float32)
    masked = coupling[0] * row_mask[:, None]
    sep_part = -product_here(subs, rows, sigma_top, coupling[0], tile_mask[0])
    update = lax.psum_scatter(
        lax.dot_general(
            masked,
            sep_part,
            (((0,), (0,)), ((), ())),
            precision=lax.Precision.HIGH,
            preferred_element_type=jnp.float32,
        ),
        "row",
        scatter_dimension=0,
        tiled=True,
    )
    block_here = child_inverse[0] - update
    own_cols = lax.dynamic_slice_in_dim(block_here, row_index * width_here, width_here, 1)
    own_diag = jnp.diagonal(own_cols)
    every_var = every_variance(subs, rows, own_diag)
    loo_var = every_var[obs_node] + obs_noise
    return (sep_part[None], block_here[None], loo_var)


def solution(mesh):
    placed = (
        P("row", "sub"),
        P("sub", "row", None),
        P("sub", "row", None),
        P("sub", None),
        P(("sub", "row")),
        P(("sub", "row")),
    )
    return jax.shard_map(
        functools.partial(local, mesh.shape["sub"], mesh.shape["row"]),
        mesh=mesh,
        in_specs=placed,
        out_specs=(P("sub", "row", None), P("sub", "row", None), P(("sub", "row"))),
        check_vma=False,
    )
```
